256 devices in a mesh: gx: 16 (over x, y_lo, core), gy: 16 (over z, y_hi).
Axes of the slice: x: 4, y: 4 (y_hi: 2, y_lo: 2; y = y_hi * 2 + y_lo), z: 8, core: 2. Of those that a mesh axis runs over, the one named last changes fastest.
Arguments:
- tensor: float32 [16, 6144, 6144], P(None, 'gx', 'gy'), may hold values from -6 to 6
- factor_b_init: float32 [6144, 128], P(('gy', 'gx')), may hold values from 0 to 1
- time_init: float32 [16, 128], replicated, may hold values from 0 to 1
Outputs:
- factor_a: float32 [6144, 128], P(('gx', 'gy'))
- factor_b: float32 [6144, 128], P(('gy', 'gx'))
- time_factor: float32 [16, 128], replicated
The draws below stay inside these ranges and needn't reach their ends.
All inputs are finite; a program needn't handle non-finite values.
Results may differ from the reference program's by a relative error of at most 0.00029.
Values sent between devices are 32-bit elements; how exact they have to be, the bound alone decides.
No kernel may reach another device: no remote copies, remote signals or barrier semaphores. Data moves between devices by JAX's collectives and lax.ppermute only.
A program may use at most 64 MiB of HBM per device.

```python
import jax
import jax.numpy as jnp
from jax import lax

K = 16
R = 128
NX = 6144
NY = 6144


def spiked(entries, rng, source, target, parts, factor):
    owner, partner = [(jnp.arange(entries.shape[position]) // (entries.shape[position] // parts)).reshape([-1 if axis == position else 1 for axis in range(entries.ndim)]) for position in (source, target)]
    chosen = jax.random.permutation(rng, parts)[partner]
    strong = (owner == chosen) | (owner == (partner + parts // 2) % parts)
    return jnp.where(strong, factor * entries, entries)


def shard_levels(stream_key, dims, shards, low, largest):
    def one(axis_at, blocks):
        heights = jax.random.uniform(jax.random.fold_in(jax.random.fold_in(stream_key, 6), axis_at), (blocks,), jnp.float32, low / len(shards), largest / len(shards))
        return jnp.repeat(jnp.exp(heights), dims[axis_at] // blocks).reshape((-1,) + (1,) * (len(dims) - axis_at - 1))

    level = one(*shards[0])
    for cut in shards[1:]:
        level = level * one(*cut)
    return level


def bell_draw_with(rng, shape, width, limit, split, heavy, dtype=jnp.bfloat16):
    result = width * jax.random.normal(rng, shape, jnp.float32)
    if split:
        result = result * shard_levels(rng, shape, split, -0.22, 0.18)
    return jnp.clip(spiked(result, jax.random.fold_in(rng, 3), *heavy), -limit, limit).astype(dtype)


def setup_inputs(seed: int = 0) -> dict:
    streams_of = jax.random.split(jax.random.key(seed), 4)
    return {
        "tensor": bell_draw_with(streams_of[0], (K, NX, NY), 1.0, 6.0, ((1, 16), (2, 16)), (2, 1, 16, 2.0), jnp.float32),
        "factor_b_init": jnp.clip(1.0 * jax.random.uniform(streams_of[1], (NY, R), jnp.float32) ** shard_levels(streams_of[1], (NY, R), ((0, 256),), -0.2, 0.2), 0.0, 1.0),
        "time_init": jnp.clip(jax.random.uniform(streams_of[2], (K, R), jnp.float32, 0.0, 1.0), 0.0, 1.0),
    }


highest = lax.Precision.HIGHEST
epsilon = 1e-06

def solve_rows(metric, rhs):
    lower = jnp.linalg.cholesky(metric)
    return jax.scipy.linalg.cho_solve((lower, True), rhs.T).T

def normalized(raw):
    gram_raw = jnp.dot(raw.T, raw, precision=highest)
    norms = jnp.sqrt(jnp.diagonal(gram_raw) + epsilon)
    return (raw / norms, gram_raw / (norms[:, None] * norms[None, :]))

def reference(tensor, factor_b_init, time_init):
    gram_time = jnp.dot(time_init.T, time_init, precision=highest)
    gram_old = jnp.dot(factor_b_init.T, factor_b_init, precision=highest)
    along_j = jnp.einsum('kij,jr->kir', tensor, factor_b_init, precision=highest)
    mttkrp_a = jnp.einsum('kir,kr->ir', along_j, time_init, precision=highest)
    unit_a, gram_a = normalized(solve_rows(gram_old * gram_time, mttkrp_a))
    along_i = jnp.einsum('kij,ir->kjr', tensor, unit_a, precision=highest)
    mttkrp_b = jnp.einsum('kjr,kr->jr', along_i, time_init, precision=highest)
    unit_b, gram_b = normalized(solve_rows(gram_a * gram_time, mttkrp_b))
    mttkrp_c = jnp.einsum('kjr,jr->kr', along_i, unit_b, precision=highest)
    time_factor = solve_rows(gram_a * gram_b, mttkrp_c)
    scale_a = jnp.sqrt(jnp.float32(unit_a.shape[0]))
    scale_b = jnp.sqrt(jnp.float32(unit_b.shape[0]))
    return (unit_a * scale_a, unit_b * scale_b, time_factor)
```

```python
import functools

import jax
import jax.numpy as jnp
from jax import lax
from jax.experimental import pallas as pl
from jax.experimental.pallas import tpu as pltpu
from jax.sharding import PartitionSpec as P

highest = lax.Precision.HIGHEST
epsilon = 1e-06
f32 = jnp.float32
bf16 = jnp.bfloat16
VMEM = pltpu.VMEM
TILE = 8


def split(x):
    high = x.astype(bf16)
    return high, (x - high.astype(f32)).astype(bf16)


def dot(a, b, ca, cb, precision=highest):
    return lax.dot_general(a, b, (((ca,), (cb,)), ((), ())), precision=precision, preferred_element_type=f32)


def raw_dot(a, b, ca, cb):
    return lax.dot_general(a, b, (((ca,), (cb,)), ((), ())), preferred_element_type=f32)


def spd_inverse(matrix):
    n = matrix.shape[0]
    blocks = n // TILE
    rows = [matrix[TILE * v : TILE * (v + 1), :] for v in range(blocks)]
    lane = lax.broadcasted_iota(jnp.int32, (TILE, n), 1)
    sub = lax.broadcasted_iota(jnp.int32, (TILE, n), 0)

    def column(value, at):
        return jnp.broadcast_to(value[:, at : at + 1], (TILE, n))

    def row(value, at):
        return jnp.broadcast_to(value[at : at + 1, :], (TILE, n))

    for block in range(blocks):
        first = TILE * block
        inside = (lane >= first) & (lane < first + TILE)
        panel = rows[block]
        columns = [column(panel, first + s) for s in range(TILE)]
        b = [[row(columns[s], i) for s in range(i + 1)] for i in range(TILE)]
        start = jnp.where(inside, jnp.where(lane - first == sub, 1.0, 0.0), panel)
        p = [row(start, i) for i in range(TILE)]
        inverse = []
        for j in range(TILE):
            inverse.append(1.0 / b[j][j])
            for i in range(j + 1, TILE):
                factor = b[i][j] * inverse[j]
                for t in range(j + 1, i + 1):
                    b[i][t] = b[i][t] - factor * b[t][j]
                p[i] = p[i] - factor * p[j]
        solved = [None] * TILE
        for j in reversed(range(TILE)):
            value = p[j]
            for i in range(j + 1, TILE):
                value = value - b[i][j] * solved[i]
            solved[j] = value * inverse[j]
        update = []
        for v in range(blocks):
            if v == block:
                value = solved[TILE - 1]
                for s in range(TILE - 1):
                    value = jnp.where(sub == s, solved[s], value)
            else:
                value = jnp.where(inside, 0.0, rows[v])
                for s in range(TILE):
                    value = value - column(rows[v], first + s) * solved[s]
            update.append(value)
        rows = update
    return jnp.concatenate(rows, axis=0)


def diagonal(matrix):
    n = matrix.shape[0]
    same = lax.broadcasted_iota(jnp.int32, (n, n), 0) == lax.broadcasted_iota(jnp.int32, (n, n), 1)
    kept = jnp.where(same, matrix, 0.0)
    return jnp.sum(kept, axis=0, keepdims=True), jnp.sum(kept, axis=1, keepdims=True)


def scaled(gram_raw):
    across, down = diagonal(gram_raw)
    norm_row, norm_column = jnp.sqrt(across + epsilon), jnp.sqrt(down + epsilon)
    return norm_row, norm_column, gram_raw / (norm_column * norm_row)


def unpack(ref, at, size):
    return jnp.concatenate([ref[s, at : at + size, :] for s in range(ref.shape[0])], axis=0)


def first_product(tensor_ref, factor_ref, time_ref, out_ref):
    factor = unpack(factor_ref, 0, factor_ref.shape[1])
    rank = factor.shape[1]
    high, low = split(factor)
    both = jnp.concatenate([high, low], axis=1)
    snapshots = tensor_ref.shape[0]
    total = jnp.zeros((tensor_ref.shape[1], rank), f32)
    for k in range(snapshots):
        t_high, t_low = split(tensor_ref[k])
        product = raw_dot(t_high, both, 1, 0)
        along = product[:, :rank] + product[:, rank:] + raw_dot(t_low, high, 1, 0)
        total = total + along * time_ref[k : k + 1, :]
    gram = dot(factor, factor, 0, 0)
    pack(out_ref, total, gram)


def pack(out_ref, total, gram):
    parts = out_ref.shape[0]
    rows, extra = total.shape[0] // parts, gram.shape[0] // parts
    for d in range(parts):
        out_ref[d, :rows, :] = total[d * rows : (d + 1) * rows]
        out_ref[d, rows:, :] = gram[d * extra : (d + 1) * extra]


def sum_and_copy(in_ref, out_ref):
    total = jnp.sum(in_ref[...], axis=0)
    for d in range(out_ref.shape[0]):
        out_ref[d] = total


def second_product(tensor_ref, in_ref, time_ref, out_ref, along_ref, raw_ref):
    rank = time_ref.shape[1]
    rows = in_ref.shape[1] - rank // in_ref.shape[0]
    time = time_ref[...]
    gram_time = dot(time, time, 0, 0)
    metric = unpack(in_ref, rows, in_ref.shape[1] - rows) * gram_time
    raw = dot(unpack(in_ref, 0, rows), spd_inverse(metric), 1, 0)
    raw_ref[...] = raw
    gram = dot(raw, raw, 0, 0)
    turned = raw.T
    high, low = split(turned)
    both = jnp.concatenate([high, low], axis=0)
    time_turned = time.T
    total = jnp.zeros((rank, tensor_ref.shape[2]), f32)
    for k in range(tensor_ref.shape[0]):
        t_high, t_low = split(tensor_ref[k])
        product = raw_dot(both, t_high, 1, 0)
        along = product[:rank] + product[rank:] + raw_dot(high, t_low, 1, 0)
        along_ref[k] = along
        total = total + along * time_turned[:, k : k + 1]
    pack(out_ref, total.T, gram)


def third_product(in_ref, along_ref, time_ref, out_ref, raw_ref, gram_ref, norm_ref):
    snapshots, rank = time_ref.shape
    rows = in_ref.shape[1] - rank // in_ref.shape[0]
    time = time_ref[...]
    gram_time = dot(time, time, 0, 0)
    norm_row, norm_column, gram_a = scaled(unpack(in_ref, rows, in_ref.shape[1] - rows))
    raw = dot(unpack(in_ref, 0, rows) / norm_row, spd_inverse(gram_a * gram_time), 1, 0)
    raw_ref[...] = raw
    gram_ref[...] = gram_a
    norm_ref[...] = norm_row
    turned = raw.T
    lane = lax.broadcasted_iota(jnp.int32, (rank, rank), 1)
    sums = jnp.zeros((rank, rank), f32)
    for k in range(snapshots):
        part = jnp.sum(along_ref[k] * turned, axis=1, keepdims=True)
        sums = jnp.where(lane == k, part, sums)
    products = (sums / norm_column).T[:snapshots]
    gram = dot(raw, raw, 0, 0)
    extra = rank // in_ref.shape[0]
    mine = gram_slice(gram, lax.axis_index("gx"), extra)
    for d in range(out_ref.shape[0]):
        out_ref[d, :snapshots, :] = products
        out_ref[d, snapshots:, :] = mine


def gram_slice(gram, index, extra):
    value = gram[:extra]
    for s in range(1, gram.shape[0] // extra):
        value = jnp.where(index == s, gram[s * extra : (s + 1) * extra], value)
    return value


def finish(size_a, size_b, in_ref, gram_a_ref, norm_a_ref, raw_a_ref, raw_b_ref, factor_a_ref, factor_b_ref, time_ref):
    snapshots = time_ref.shape[0]
    norm_row, _, gram_b = scaled(unpack(in_ref, snapshots, in_ref.shape[1] - snapshots))
    products = jnp.sum(in_ref[:, :snapshots, :], axis=0) / norm_row
    time_ref[...] = dot(products, spd_inverse(gram_a_ref[...] * gram_b), 1, 0)
    rows_a, rows_b = factor_a_ref.shape[0], factor_b_ref.shape[0]
    at_a = pl.multiple_of(lax.axis_index("gy") * rows_a, TILE)
    at_b = pl.multiple_of(lax.axis_index("gx") * rows_b, TILE)
    factor_a_ref[...] = raw_a_ref[pl.ds(at_a, rows_a), :] / norm_a_ref[...] * jnp.sqrt(f32(size_a))
    factor_b_ref[...] = raw_b_ref[pl.ds(at_b, rows_b), :] / norm_row * jnp.sqrt(f32(size_b))


def call(kernel, inputs, outputs, name, limit=48 << 20):
    shapes = [jax.ShapeDtypeStruct(s, f32) for s in outputs]
    single = len(shapes) == 1
    space = pl.BlockSpec(memory_space=VMEM)
    return pl.pallas_call(
        kernel,
        out_shape=shapes[0] if single else shapes,
        in_specs=[space] * len(inputs),
        out_specs=space if single else [space] * len(shapes),
        compiler_params=pltpu.CompilerParams(vmem_limit_bytes=limit),
        name=name,
    )(*inputs)


def exchange(value, axis):
    return lax.all_to_all(value, axis, 0, 0)


def shards(tensor, factor_b_init, time_init):
    nx, ny = lax.axis_size("gx"), lax.axis_size("gy")
    snapshots, rank = time_init.shape
    rows_i, rows_j = tensor.shape[1], tensor.shape[2]
    own_i, own_j = rows_i // ny, rows_j // nx
    extra_x, extra_y = rank // nx, rank // ny
    block_b = exchange(jnp.broadcast_to(factor_b_init[None], (nx,) + factor_b_init.shape), "gx")
    sent = call(first_product, (tensor, block_b, time_init), [(ny, own_i + extra_y, rank)], "first_product")
    sent = exchange(sent, "gy")
    sent = call(sum_and_copy, (sent,), [sent.shape], "sum_a")
    sent = exchange(sent, "gy")
    sent, along, raw_a = call(
        second_product,
        (tensor, sent, time_init),
        [(nx, own_j + extra_x, rank), (snapshots, rank, rows_j), (rows_i, rank)],
        "second_product",
    )
    sent = exchange(sent, "gx")
    sent = call(sum_and_copy, (sent,), [sent.shape], "sum_b")
    sent = exchange(sent, "gx")
    sent, raw_b, gram_a, norm_a = call(
        third_product,
        (sent, along, time_init),
        [(ny, snapshots + extra_x, rank), (rows_j, rank), (rank, rank), (1, rank)],
        "third_product",
    )
    sent = exchange(sent, "gy")
    sent = call(sum_and_copy, (sent,), [(nx,) + sent.shape[1:]], "sum_c")
    sent = exchange(sent, "gx")
    return call(
        functools.partial(finish, rows_i * nx, rows_j * ny),
        (sent, gram_a, norm_a, raw_a, raw_b),
        [(own_i, rank), (own_j, rank), (snapshots, rank)],
        "finish",
    )


def solution(mesh):
    return jax.shard_map(
        lambda *arrays: tuple(shards(*arrays)),
        mesh=mesh,
        in_specs=(P(None, "gx", "gy"), P(("gy", "gx"), None), P()),
        out_specs=(P(("gx", "gy"), None), P(("gy", "gx"), None), P()),
        check_vma=False,
    )
```

```python
import functools

import jax
import jax.numpy as jnp
from jax import lax
from jax.experimental import pallas as pl
from jax.experimental.pallas import tpu as pltpu
from jax.sharding import PartitionSpec as P

highest = lax.Precision.HIGHEST
epsilon = 1e-06
f32 = jnp.float32
bf16 = jnp.bfloat16
VMEM = pltpu.VMEM
TILE = 8
PAIR = 2


def split(x):
    high = x.astype(bf16)
    return high, (x - high.astype(f32)).astype(bf16)


def dot(a, b, ca, cb, precision=highest):
    return lax.dot_general(a, b, (((ca,), (cb,)), ((), ())), precision=precision, preferred_element_type=f32)


def raw_dot(a, b, ca, cb):
    return lax.dot_general(a, b, (((ca,), (cb,)), ((), ())), preferred_element_type=f32)


def spd_inverse(matrix):
    n = matrix.shape[0]
    blocks = n // TILE
    rows = [matrix[TILE * v : TILE * (v + 1), :] for v in range(blocks)]
    lane = lax.broadcasted_iota(jnp.int32, (TILE, n), 1)
    sub = lax.broadcasted_iota(jnp.int32, (TILE, n), 0)

    def column(value, at):
        return jnp.take_along_axis(value, jnp.full((TILE, n), at, jnp.int32), axis=1)

    def row(value, at):
        return jnp.broadcast_to(value[at : at + 1, :], (TILE, n))

    for block in range(blocks):
        first = TILE * block
        inside = (lane >= first) & (lane < first + TILE)
        panel = rows[block]
        columns = [column(panel, first + s) for s in range(TILE)]
        b = [[row(columns[s], i) for s in range(i + 1)] for i in range(TILE)]
        start = jnp.where(inside, jnp.where(lane - first == sub, 1.0, 0.0), panel)
        p = [row(start, i) for i in range(TILE)]
        inverse = []
        for j in range(TILE):
            inverse.append(1.0 / b[j][j])
            for i in range(j + 1, TILE):
                factor = b[i][j] * inverse[j]
                for t in range(j + 1, i + 1):
                    b[i][t] = b[i][t] - factor * b[t][j]
                p[i] = p[i] - factor * p[j]
        solved = [None] * TILE
        for j in reversed(range(TILE)):
            value = p[j]
            for i in range(j + 1, TILE):
                value = value - b[i][j] * solved[i]
            solved[j] = value * inverse[j]
        update = []
        for v in range(blocks):
            if v == block:
                value = solved[TILE - 1]
                for s in range(TILE - 1):
                    value = jnp.where(sub == s, solved[s], value)
            else:
                value = jnp.where(inside, 0.0, rows[v])
                for s in range(TILE):
                    value = value - column(rows[v], first + s) * solved[s]
            update.append(value)
        rows = update
    return jnp.concatenate(rows, axis=0)


def diagonal(matrix):
    n = matrix.shape[0]
    same = lax.broadcasted_iota(jnp.int32, (n, n), 0) == lax.broadcasted_iota(jnp.int32, (n, n), 1)
    kept = jnp.where(same, matrix, 0.0)
    return jnp.sum(kept, axis=0, keepdims=True), jnp.sum(kept, axis=1, keepdims=True)


def metric_inverse(metric):
    across, down = diagonal(metric)
    scale = lax.rsqrt(across) * lax.rsqrt(down)
    return spd_inverse(metric * scale) * scale


def scaled(gram_raw):
    across, down = diagonal(gram_raw)
    norm_row, norm_column = jnp.sqrt(across + epsilon), jnp.sqrt(down + epsilon)
    return norm_row, norm_column, gram_raw / (norm_column * norm_row)


def unpack(ref, at, size):
    return jnp.concatenate([ref[s, at : at + size, :] for s in range(ref.shape[0])], axis=0)


def spread(factor_ref, time_ref, out_ref, time_out_ref):
    for d in range(out_ref.shape[0]):
        out_ref[d] = factor_ref[...]
    time_out_ref[...] = time_ref[...]


def first_product(tensor_ref, factor_ref, time_ref, out_ref, high_ref, low_ref, held, arrived):
    copies = [pltpu.make_async_copy(tensor_ref.at[k], held.at[k], arrived.at[k]) for k in range(held.shape[0])]
    for copy in copies:
        copy.start()
    factor = unpack(factor_ref, 0, factor_ref.shape[1])
    columns, rank = factor.shape
    total = jnp.zeros((tensor_ref.shape[1], rank), f32)
    for first in range(0, time_ref.shape[0], PAIR):
        weights = jnp.concatenate([factor * time_ref[k : k + 1, :] for k in range(first, first + PAIR)], axis=0)
        high, low = split(weights)
        both = jnp.concatenate([high, low], axis=1)
        for k in range(first, first + PAIR):
            copies[k].wait()
        t_high, t_low = split(jnp.concatenate([held[k] for k in range(first, first + PAIR)], axis=1))
        at = first * columns
        high_ref[:, at : at + PAIR * columns] = t_high
        low_ref[:, at : at + PAIR * columns] = t_low
        product = raw_dot(t_high, both, 1, 0)
        total = total + (product[:, :rank] + product[:, rank:] + raw_dot(t_low, high, 1, 0))
    gram = dot(factor, factor, 0, 0)
    pack(out_ref, total, gram)


def pack(out_ref, total, gram):
    parts = out_ref.shape[0]
    rows, extra = total.shape[0] // parts, gram.shape[0] // parts
    for d in range(parts):
        out_ref[d, :rows, :] = total[d * rows : (d + 1) * rows]
        out_ref[d, rows:, :] = gram[d * extra : (d + 1) * extra]


def sum_and_copy(in_ref, out_ref):
    total = jnp.sum(in_ref[...], axis=0)
    for d in range(out_ref.shape[0]):
        out_ref[d] = total


def second_product(high_ref, low_ref, in_ref, time_ref, out_ref, along_ref, raw_ref):
    snapshots, rank = time_ref.shape
    rows = in_ref.shape[1] - rank // in_ref.shape[0]
    time = time_ref[...]
    gram_time = dot(time, time, 0, 0)
    metric = unpack(in_ref, rows, in_ref.shape[1] - rows) * gram_time
    raw = dot(unpack(in_ref, 0, rows), metric_inverse(metric), 1, 0)
    raw_ref[...] = raw
    turned = raw.T
    gram = dot(turned, raw, 1, 0)
    high, low = split(turned)
    both = jnp.concatenate([high, low], axis=0)
    time_turned = time.T
    columns = high_ref.shape[1] // snapshots
    wide = PAIR * columns
    total = jnp.zeros((rank, columns), f32)
    for first in range(0, snapshots, PAIR):
        at = first * columns
        product = raw_dot(both, high_ref[:, at : at + wide], 1, 0)
        along = product[:rank] + product[rank:] + raw_dot(high, low_ref[:, at : at + wide], 1, 0)
        along_ref[:, at : at + wide] = along
        for k in range(PAIR):
            total = total + along[:, k * columns : (k + 1) * columns] * time_turned[:, first + k : first + k + 1]
    pack(out_ref, total.T, gram)


def third_product(in_ref, along_ref, time_ref, out_ref, raw_ref, gram_ref, norm_ref):
    snapshots, rank = time_ref.shape
    rows = in_ref.shape[1] - rank // in_ref.shape[0]
    time = time_ref[...]
    gram_time = dot(time, time, 0, 0)
    norm_row, norm_column, gram_a = scaled(unpack(in_ref, rows, in_ref.shape[1] - rows))
    raw = dot(unpack(in_ref, 0, rows) / norm_row, metric_inverse(gram_a * gram_time), 1, 0)
    raw_ref[...] = raw
    gram_ref[...] = gram_a
    norm_ref[...] = norm_row
    turned = raw.T
    columns = raw.shape[0]
    lane = lax.broadcasted_iota(jnp.int32, (rank, rank), 1)
    sums = jnp.zeros((rank, rank), f32)
    for k in range(snapshots):
        part = jnp.sum(along_ref[:, k * columns : (k + 1) * columns] * turned, axis=1, keepdims=True)
        sums = jnp.where(lane == k, part, sums)
    products = (sums / norm_column).T[:snapshots]
    gram = dot(turned, raw, 1, 0)
    extra = rank // in_ref.shape[0]
    mine = gram_slice(gram, lax.axis_index("gx"), extra)
    for d in range(out_ref.shape[0]):
        out_ref[d, :snapshots, :] = products
        out_ref[d, snapshots:, :] = mine


def gram_slice(gram, index, extra):
    value = gram[:extra]
    for s in range(1, gram.shape[0] // extra):
        value = jnp.where(index == s, gram[s * extra : (s + 1) * extra], value)
    return value


def finish(size_a, size_b, in_ref, gram_a_ref, norm_a_ref, raw_a_ref, raw_b_ref, factor_a_ref, factor_b_ref, time_ref):
    snapshots = time_ref.shape[0]
    norm_row, _, gram_b = scaled(unpack(in_ref, snapshots, in_ref.shape[1] - snapshots))
    products = jnp.sum(in_ref[:, :snapshots, :], axis=0) / norm_row
    time_ref[...] = dot(products, metric_inverse(gram_a_ref[...] * gram_b), 1, 0)
    rows_a, rows_b = factor_a_ref.shape[0], factor_b_ref.shape[0]
    at_a = pl.multiple_of(lax.axis_index("gy") * rows_a, TILE)
    at_b = pl.multiple_of(lax.axis_index("gx") * rows_b, TILE)
    factor_a_ref[...] = raw_a_ref[pl.ds(at_a, rows_a), :] / norm_a_ref[...] * jnp.sqrt(f32(size_a))
    factor_b_ref[...] = raw_b_ref[pl.ds(at_b, rows_b), :] / norm_row * jnp.sqrt(f32(size_b))


def call(kernel, inputs, outputs, name, spaces=None, scratch=(), limit=16 << 20):
    shapes = [o if isinstance(o, jax.ShapeDtypeStruct) else jax.ShapeDtypeStruct(o, f32) for o in outputs]
    single = len(shapes) == 1
    space = pl.BlockSpec(memory_space=VMEM)
    return pl.pallas_call(
        kernel,
        out_shape=shapes[0] if single else shapes,
        in_specs=spaces or [space] * len(inputs),
        out_specs=space if single else [space] * len(shapes),
        scratch_shapes=scratch,
        compiler_params=pltpu.CompilerParams(vmem_limit_bytes=limit),
        name=name,
    )(*inputs)


def exchange(value, axis):
    return lax.all_to_all(value, axis, 0, 0)


def shards(tensor, factor_b_init, time_init):
    nx, ny = lax.axis_size("gx"), lax.axis_size("gy")
    snapshots, rank = time_init.shape
    rows_i, rows_j = tensor.shape[1], tensor.shape[2]
    own_i, own_j = rows_i // ny, rows_j // nx
    extra_x, extra_y = rank // nx, rank // ny
    block_b, time = call(spread, (factor_b_init, time_init), [(nx,) + factor_b_init.shape, time_init.shape], "spread")
    block_b = exchange(block_b, "gx")
    half = jax.ShapeDtypeStruct((rows_i, snapshots * rows_j), bf16)
    space = pl.BlockSpec(memory_space=VMEM)
    sent, high, low = call(
        first_product,
        (tensor, block_b, time),
        [(ny, own_i + extra_y, rank), half, half],
        "first_product",
        [pl.BlockSpec(memory_space=pl.ANY), space, space],
        [VMEM(tensor.shape, f32), pltpu.SemaphoreType.DMA((snapshots,))],
        42 << 20,
    )
    sent = exchange(sent, "gy")
    sent = call(sum_and_copy, (sent,), [sent.shape], "sum_a")
    sent = exchange(sent, "gy")
    sent, along, raw_a = call(
        second_product,
        (high, low, sent, time),
        [(nx, own_j + extra_x, rank), (rank, snapshots * rows_j), (rows_i, rank)],
        "second_product",
    )
    sent = exchange(sent, "gx")
    sent = call(sum_and_copy, (sent,), [sent.shape], "sum_b")
    sent = exchange(sent, "gx")
    sent, raw_b, gram_a, norm_a = call(
        third_product,
        (sent, along, time),
        [(ny, snapshots + extra_x, rank), (rows_j, rank), (rank, rank), (1, rank)],
        "third_product",
    )
    sent = exchange(sent, "gy")
    sent = call(sum_and_copy, (sent,), [(nx,) + sent.shape[1:]], "sum_c")
    sent = exchange(sent, "gx")
    return call(
        functools.partial(finish, rows_i * nx, rows_j * ny),
        (sent, gram_a, norm_a, raw_a, raw_b),
        [(own_i, rank), (own_j, rank), (snapshots, rank)],
        "finish",
    )


def solution(mesh):
    return jax.shard_map(
        lambda *arrays: tuple(shards(*arrays)),
        mesh=mesh,
        in_specs=(P(None, "gx", "gy"), P(("gy", "gx"), None), P()),
        out_specs=(P(("gx", "gy"), None), P(("gy", "gx"), None), P()),
        check_vma=False,
    )
```

```python
import functools

import jax
import jax.numpy as jnp
from jax import lax
from jax.experimental import pallas as pl
from jax.experimental.pallas import tpu as pltpu
from jax.sharding import PartitionSpec as P

highest = lax.Precision.HIGHEST
epsilon = 1e-06
f32 = jnp.float32
bf16 = jnp.bfloat16
VMEM = pltpu.VMEM
TILE = 8
PAIR = 2
LOOK = 2


def split(x):
    high = x.astype(bf16)
    return high, (x - high.astype(f32)).astype(bf16)


def dot(a, b, ca, cb, precision=highest):
    return lax.dot_general(a, b, (((ca,), (cb,)), ((), ())), precision=precision, preferred_element_type=f32)


def raw_dot(a, b, ca, cb):
    return lax.dot_general(a, b, (((ca,), (cb,)), ((), ())), preferred_element_type=f32)


def three_parts(x):
    high = x.astype(bf16)
    rest = x - high.astype(f32)
    middle = rest.astype(bf16)
    return high, middle, (rest - middle.astype(f32)).astype(bf16)


def spd_inverse(matrix):
    n = matrix.shape[0]
    blocks = n // TILE
    rows = [matrix[TILE * v : TILE * (v + 1), :] for v in range(blocks)]
    lane = lax.broadcasted_iota(jnp.int32, (TILE, n), 1)
    sub = lax.broadcasted_iota(jnp.int32, (TILE, n), 0)
    zero = jnp.zeros((TILE, n), f32)

    def column(value, at):
        return jnp.take_along_axis(value, jnp.full((TILE, n), at, jnp.int32), axis=1)

    def row(value, at):
        return jnp.broadcast_to(value[at : at + 1, :], (TILE, n))

    for block in range(blocks):
        first = TILE * block
        inside = (lane >= first) & (lane < first + TILE)
        panel = rows[block]
        columns = [column(panel, first + s) for s in range(TILE)]
        b = [[row(columns[s], i) for s in range(i + 1)] for i in range(TILE)]
        start = jnp.where(inside, jnp.where(lane - first == sub, 1.0, 0.0), panel)
        p = [row(start, i) for i in range(TILE)]
        inverse = []
        for j in range(TILE):
            inverse.append(1.0 / b[j][j])
            for i in range(j + 1, TILE):
                factor = b[i][j] * inverse[j]
                for t in range(j + 1, i + 1):
                    b[i][t] = b[i][t] - factor * b[t][j]
                p[i] = p[i] - factor * p[j]
        solved = [None] * TILE
        for j in reversed(range(TILE)):
            value = p[j]
            for i in range(j + 1, TILE):
                value = value - b[i][j] * solved[i]
            solved[j] = value * inverse[j]
        result = solved[TILE - 1]
        for s in range(TILE - 1):
            result = jnp.where(sub == s, solved[s], result)
        c_high, c_middle, c_low = three_parts(jnp.concatenate(rows, axis=0))
        padded = jnp.concatenate([result if v == block else zero for v in range(blocks)], axis=0)
        r_high, r_middle, r_low = three_parts(padded)
        pair = jnp.concatenate([r_high, r_middle], axis=1)
        large = raw_dot(jnp.concatenate([c_high, c_middle], axis=1), jnp.concatenate([pair, pair], axis=0), 1, 0)
        small = raw_dot(jnp.concatenate([c_high, c_low], axis=1), jnp.concatenate([r_low, r_high], axis=0), 1, 0)
        product = large[:, :n] + (large[:, n:] + small)
        near = [(block + 1 + q) % blocks for q in range(LOOK)]
        update = []
        for v in range(blocks):
            if v == block:
                update.append(result)
                continue
            if v in near:
                terms = [column(rows[v], first + s) * solved[s] for s in range(TILE)]
                while len(terms) > 1:
                    terms = [terms[q] + terms[q + 1] for q in range(0, len(terms), 2)]
                change = terms[0]
            else:
                change = product[TILE * v : TILE * (v + 1), :]
            update.append(jnp.where(inside, 0.0, rows[v]) - change)
        rows = update
    return jnp.concatenate(rows, axis=0)


def diagonal(matrix):
    n = matrix.shape[0]
    same = lax.broadcasted_iota(jnp.int32, (n, n), 0) == lax.broadcasted_iota(jnp.int32, (n, n), 1)
    kept = jnp.where(same, matrix, 0.0)
    return jnp.sum(kept, axis=0, keepdims=True), jnp.sum(kept, axis=1, keepdims=True)


def metric_inverse(metric):
    across, down = diagonal(metric)
    scale = lax.rsqrt(across) * lax.rsqrt(down)
    return spd_inverse(metric * scale) * scale


def scaled(gram_raw):
    across, down = diagonal(gram_raw)
    norm_row, norm_column = jnp.sqrt(across + epsilon), jnp.sqrt(down + epsilon)
    return norm_row, norm_column, gram_raw / (norm_column * norm_row)


def unpack(ref, at, size):
    return jnp.concatenate([ref[s, at : at + size, :] for s in range(ref.shape[0])], axis=0)


def spread(factor_ref, out_ref):
    for d in range(out_ref.shape[0]):
        out_ref[d] = factor_ref[...]


def first_product(tensor_ref, factor_ref, time_ref, out_ref, high_ref, low_ref):
    factor = unpack(factor_ref, 0, factor_ref.shape[1])
    columns, rank = factor.shape
    total = jnp.zeros((tensor_ref.shape[1], rank), f32)
    for first in range(0, time_ref.shape[0], PAIR):
        weights = jnp.concatenate([factor * time_ref[k : k + 1, :] for k in range(first, first + PAIR)], axis=0)
        high, low = split(weights)
        both = jnp.concatenate([high, low], axis=1)
        t_high, t_low = split(jnp.concatenate([tensor_ref[k] for k in range(first, first + PAIR)], axis=1))
        at = first * columns
        high_ref[:, at : at + PAIR * columns] = t_high
        low_ref[:, at : at + PAIR * columns] = t_low
        product = raw_dot(t_high, both, 1, 0)
        total = total + (product[:, :rank] + product[:, rank:] + raw_dot(t_low, high, 1, 0))
    gram = dot(factor, factor, 0, 0)
    pack(out_ref, total, gram)


def pack(out_ref, total, gram):
    parts = out_ref.shape[0]
    rows, extra = total.shape[0] // parts, gram.shape[0] // parts
    for d in range(parts):
        out_ref[d, :rows, :] = total[d * rows : (d + 1) * rows]
        out_ref[d, rows:, :] = gram[d * extra : (d + 1) * extra]


def sum_and_copy(in_ref, out_ref):
    total = jnp.sum(in_ref[...], axis=0)
    for d in range(out_ref.shape[0]):
        out_ref[d] = total


def second_product(high_ref, low_ref, in_ref, time_ref, out_ref, along_ref, raw_ref):
    snapshots, rank = time_ref.shape
    rows = in_ref.shape[1] - rank // in_ref.shape[0]
    time = time_ref[...]
    gram_time = dot(time, time, 0, 0)
    metric = unpack(in_ref, rows, in_ref.shape[1] - rows) * gram_time
    raw = dot(unpack(in_ref, 0, rows), metric_inverse(metric), 1, 0)
    raw_ref[...] = raw
    turned = raw.T
    gram = dot(turned, raw, 1, 0)
    high, low = split(turned)
    both = jnp.concatenate([high, low], axis=0)
    time_turned = time.T
    columns = high_ref.shape[1] // snapshots
    wide = PAIR * columns
    total = jnp.zeros((rank, columns), f32)
    for first in range(0, snapshots, PAIR):
        at = first * columns
        product = raw_dot(both, high_ref[:, at : at + wide], 1, 0)
        along = product[:rank] + product[rank:] + raw_dot(high, low_ref[:, at : at + wide], 1, 0)
        along_ref[:, at : at + wide] = along
        for k in range(PAIR):
            total = total + along[:, k * columns : (k + 1) * columns] * time_turned[:, first + k : first + k + 1]
    pack(out_ref, total.T, gram)


def third_product(in_ref, along_ref, time_ref, out_ref, raw_ref, gram_ref, norm_ref):
    snapshots, rank = time_ref.shape
    rows = in_ref.shape[1] - rank // in_ref.shape[0]
    time = time_ref[...]
    gram_time = dot(time, time, 0, 0)
    norm_row, norm_column, gram_a = scaled(unpack(in_ref, rows, in_ref.shape[1] - rows))
    raw = dot(unpack(in_ref, 0, rows) / norm_row, metric_inverse(gram_a * gram_time), 1, 0)
    raw_ref[...] = raw
    gram_ref[...] = gram_a
    norm_ref[...] = norm_row
    turned = raw.T
    columns = raw.shape[0]
    lane = lax.broadcasted_iota(jnp.int32, (rank, rank), 1)
    sums = jnp.zeros((rank, rank), f32)
    for k in range(snapshots):
        part = jnp.sum(along_ref[:, k * columns : (k + 1) * columns] * turned, axis=1, keepdims=True)
        sums = jnp.where(lane == k, part, sums)
    products = (sums / norm_column).T[:snapshots]
    gram = dot(turned, raw, 1, 0)
    extra = rank // in_ref.shape[0]
    mine = gram_slice(gram, lax.axis_index("gx"), extra)
    for d in range(out_ref.shape[0]):
        out_ref[d, :snapshots, :] = products
        out_ref[d, snapshots:, :] = mine


def gram_slice(gram, index, extra):
    value = gram[:extra]
    for s in range(1, gram.shape[0] // extra):
        value = jnp.where(index == s, gram[s * extra : (s + 1) * extra], value)
    return value


def finish(size_a, size_b, in_ref, gram_a_ref, norm_a_ref, raw_a_ref, raw_b_ref, factor_a_ref, factor_b_ref, time_ref):
    snapshots = time_ref.shape[0]
    norm_row, _, gram_b = scaled(unpack(in_ref, snapshots, in_ref.shape[1] - snapshots))
    products = jnp.sum(in_ref[:, :snapshots, :], axis=0) / norm_row
    time_ref[...] = dot(products, metric_inverse(gram_a_ref[...] * gram_b), 1, 0)
    rows_a, rows_b = factor_a_ref.shape[0], factor_b_ref.shape[0]
    at_a = pl.multiple_of(lax.axis_index("gy") * rows_a, TILE)
    at_b = pl.multiple_of(lax.axis_index("gx") * rows_b, TILE)
    factor_a_ref[...] = raw_a_ref[pl.ds(at_a, rows_a), :] / norm_a_ref[...] * jnp.sqrt(f32(size_a))
    factor_b_ref[...] = raw_b_ref[pl.ds(at_b, rows_b), :] / norm_row * jnp.sqrt(f32(size_b))


def call(kernel, inputs, outputs, name, spaces=None, scratch=(), limit=16 << 20, cost=None):
    shapes = [o if isinstance(o, jax.ShapeDtypeStruct) else jax.ShapeDtypeStruct(o, f32) for o in outputs]
    single = len(shapes) == 1
    space = pl.BlockSpec(memory_space=VMEM)
    return pl.pallas_call(
        kernel,
        out_shape=shapes[0] if single else shapes,
        in_specs=spaces or [space] * len(inputs),
        out_specs=space if single else [space] * len(shapes),
        scratch_shapes=scratch,
        cost_estimate=cost,
        compiler_params=pltpu.CompilerParams(vmem_limit_bytes=limit),
        name=name,
    )(*inputs)


def exchange(value, axis):
    return lax.all_to_all(value, axis, 0, 0)


def shards(tensor, factor_b_init, time_init):
    nx, ny = lax.axis_size("gx"), lax.axis_size("gy")
    snapshots, rank = time_init.shape
    rows_i, rows_j = tensor.shape[1], tensor.shape[2]
    own_i, own_j = rows_i // ny, rows_j // nx
    extra_x, extra_y = rank // nx, rank // ny
    behind = pl.CostEstimate(flops=5 * 10**9, bytes_accessed=2 * factor_b_init.size * 4 * nx, transcendentals=0)
    block_b = call(spread, (factor_b_init,), [(nx,) + factor_b_init.shape], "spread", cost=behind)
    block_b = exchange(block_b, "gx")
    half = jax.ShapeDtypeStruct((rows_i, snapshots * rows_j), bf16)
    sent, high, low = call(
        first_product,
        (tensor, block_b, time_init),
        [(ny, own_i + extra_y, rank), half, half],
        "first_product",
        limit=16 << 20,
    )
    sent = exchange(sent, "gy")
    sent = call(sum_and_copy, (sent,), [sent.shape], "sum_a")
    sent = exchange(sent, "gy")
    sent, along, raw_a = call(
        second_product,
        (high, low, sent, time_init),
        [(nx, own_j + extra_x, rank), (rank, snapshots * rows_j), (rows_i, rank)],
        "second_product",
    )
    sent = exchange(sent, "gx")
    sent = call(sum_and_copy, (sent,), [sent.shape], "sum_b")
    sent = exchange(sent, "gx")
    sent, raw_b, gram_a, norm_a = call(
        third_product,
        (sent, along, time_init),
        [(ny, snapshots + extra_x, rank), (rows_j, rank), (rank, rank), (1, rank)],
        "third_product",
    )
    sent = exchange(sent, "gy")
    sent = call(sum_and_copy, (sent,), [(nx,) + sent.shape[1:]], "sum_c")
    sent = exchange(sent, "gx")
    return call(
        functools.partial(finish, rows_i * nx, rows_j * ny),
        (sent, gram_a, norm_a, raw_a, raw_b),
        [(own_i, rank), (own_j, rank), (snapshots, rank)],
        "finish",
    )


def solution(mesh):
    return jax.shard_map(
        lambda *arrays: tuple(shards(*arrays)),
        mesh=mesh,
        in_specs=(P(None, "gx", "gy"), P(("gy", "gx"), None), P()),
        out_specs=(P(("gx", "gy"), None), P(("gy", "gx"), None), P()),
        check_vma=False,
    )
```

```python
import functools

import jax
import jax.numpy as jnp
from jax import lax
from jax.experimental import pallas as pl
from jax.experimental.pallas import tpu as pltpu
from jax.sharding import PartitionSpec as P

highest = lax.Precision.HIGHEST
epsilon = 1e-06
f32 = jnp.float32
bf16 = jnp.bfloat16
VMEM = pltpu.VMEM
TILE = 8
PAIR = 2
LOOK = 2


def split(x):
    high = x.astype(bf16)
    return high, (x - high.astype(f32)).astype(bf16)


def dot(a, b, ca, cb, precision=highest):
    return lax.dot_general(a, b, (((ca,), (cb,)), ((), ())), precision=precision, preferred_element_type=f32)


def raw_dot(a, b, ca, cb):
    return lax.dot_general(a, b, (((ca,), (cb,)), ((), ())), preferred_element_type=f32)


def three_parts(x):
    high = x.astype(bf16)
    rest = x - high.astype(f32)
    middle = rest.astype(bf16)
    return high, middle, (rest - middle.astype(f32)).astype(bf16)


def spd_inverse(matrix):
    n = matrix.shape[0]
    blocks = n // TILE
    rows = [matrix[TILE * v : TILE * (v + 1), :] for v in range(blocks)]
    lane = lax.broadcasted_iota(jnp.int32, (TILE, n), 1)
    sub = lax.broadcasted_iota(jnp.int32, (TILE, n), 0)
    zero = jnp.zeros((TILE, n), f32)

    def column(value, at):
        return jnp.take_along_axis(value, jnp.full((TILE, n), at, jnp.int32), axis=1)

    def row(value, at):
        return jnp.broadcast_to(value[at : at + 1, :], (TILE, n))

    for block in range(blocks):
        first = TILE * block
        inside = (lane >= first) & (lane < first + TILE)
        panel = rows[block]
        columns = [column(panel, first + s) for s in range(TILE)]
        b = [[row(columns[s], i) for s in range(i + 1)] for i in range(TILE)]
        start = jnp.where(inside, jnp.where(lane - first == sub, 1.0, 0.0), panel)
        p = [row(start, i) for i in range(TILE)]
        inverse = []
        for j in range(TILE):
            inverse.append(1.0 / b[j][j])
            for i in range(j + 1, TILE):
                factor = b[i][j] * inverse[j]
                for t in range(j + 1, i + 1):
                    b[i][t] = b[i][t] - factor * b[t][j]
                p[i] = p[i] - factor * p[j]
        solved = [None] * TILE
        for j in reversed(range(TILE)):
            value = p[j]
            for i in range(j + 1, TILE):
                value = value - b[i][j] * solved[i]
            solved[j] = value * inverse[j]
        result = solved[TILE - 1]
        for s in range(TILE - 1):
            result = jnp.where(sub == s, solved[s], result)
        c_high, c_middle, c_low = three_parts(jnp.concatenate(rows, axis=0))
        r_high, r_middle, r_low = [
            jnp.concatenate([part.astype(f32) if v == block else zero for v in range(blocks)], axis=0).astype(bf16)
            for part in three_parts(result)
        ]
        pair = jnp.concatenate([r_high, r_middle], axis=1)
        large = raw_dot(jnp.concatenate([c_high, c_middle], axis=1), jnp.concatenate([pair, pair], axis=0), 1, 0)
        small = raw_dot(jnp.concatenate([c_high, c_low], axis=1), jnp.concatenate([r_low, r_high], axis=0), 1, 0)
        product = large[:, :n] + (large[:, n:] + small)
        near = [(block + 1 + q) % blocks for q in range(LOOK)]
        update = []
        for v in range(blocks):
            if v == block:
                update.append(result)
                continue
            if v in near:
                terms = [column(rows[v], first + s) * solved[s] for s in range(TILE)]
                while len(terms) > 1:
                    terms = [terms[q] + terms[q + 1] for q in range(0, len(terms), 2)]
                change = terms[0]
            else:
                change = product[TILE * v : TILE * (v + 1), :]
            update.append(jnp.where(inside, 0.0, rows[v]) - change)
        rows = update
    return jnp.concatenate(rows, axis=0)


def diagonal(matrix):
    n = matrix.shape[0]
    same = lax.broadcasted_iota(jnp.int32, (n, n), 0) == lax.broadcasted_iota(jnp.int32, (n, n), 1)
    kept = jnp.where(same, matrix, 0.0)
    return jnp.sum(kept, axis=0, keepdims=True), jnp.sum(kept, axis=1, keepdims=True)


def metric_inverse(one, other, one_diagonal, other_diagonal):
    across, down = [lax.rsqrt(p * q) for p, q in zip(one_diagonal, other_diagonal)]
    scale = down * across
    return spd_inverse(one * other * scale) * scale


def scaled(gram_raw):
    across, down = diagonal(gram_raw)
    norm_row, norm_column = jnp.sqrt(across + epsilon), jnp.sqrt(down + epsilon)
    ends = across / (norm_row * norm_row), down / (norm_column * norm_column)
    return norm_row, norm_column, gram_raw / (norm_column * norm_row), ends


def unpack(ref, at, size):
    return jnp.concatenate([ref[s, at : at + size, :] for s in range(ref.shape[0])], axis=0)


def spread(factor_ref, out_ref):
    for d in range(out_ref.shape[0]):
        out_ref[d] = factor_ref[...]


def first_product(tensor_ref, factor_ref, time_ref, out_ref, high_ref, low_ref, gram_time_ref):
    factor = unpack(factor_ref, 0, factor_ref.shape[1])
    columns, rank = factor.shape
    total = jnp.zeros((tensor_ref.shape[1], rank), f32)
    for first in range(0, time_ref.shape[0], PAIR):
        weights = jnp.concatenate([factor * time_ref[k : k + 1, :] for k in range(first, first + PAIR)], axis=0)
        high, low = split(weights)
        both = jnp.concatenate([high, low], axis=1)
        t_high, t_low = split(jnp.concatenate([tensor_ref[k] for k in range(first, first + PAIR)], axis=1))
        at = first * columns
        high_ref[:, at : at + PAIR * columns] = t_high
        low_ref[:, at : at + PAIR * columns] = t_low
        product = raw_dot(t_high, both, 1, 0)
        total = total + (product[:, :rank] + product[:, rank:] + raw_dot(t_low, high, 1, 0))
    gram = dot(factor, factor, 0, 0)
    pack(out_ref, total, gram)
    gram_time_ref[...] = dot(time_ref[...], time_ref[...], 0, 0)


def pack(out_ref, total, gram):
    parts = out_ref.shape[0]
    rows, extra = total.shape[0] // parts, gram.shape[0] // parts
    for d in range(parts):
        out_ref[d, :rows, :] = total[d * rows : (d + 1) * rows]
        out_ref[d, rows:, :] = gram[d * extra : (d + 1) * extra]


def sum_and_copy(in_ref, out_ref):
    total = jnp.sum(in_ref[...], axis=0)
    for d in range(out_ref.shape[0]):
        out_ref[d] = total


def second_product(high_ref, low_ref, in_ref, time_ref, gram_time_ref, out_ref, along_ref, raw_ref):
    snapshots, rank = time_ref.shape
    rows = in_ref.shape[1] - rank // in_ref.shape[0]
    gram_old, gram_time = unpack(in_ref, rows, in_ref.shape[1] - rows), gram_time_ref[...]
    inverse = metric_inverse(gram_old, gram_time, diagonal(gram_old), diagonal(gram_time))
    turned = dot(inverse, unpack(in_ref, 0, rows), 1, 1)
    raw_ref[...] = dot(in_ref[lax.axis_index("gy"), :rows, :], inverse, 1, 1)
    gram = dot(turned, turned, 1, 1)
    high, low = split(turned)
    both = jnp.concatenate([high, low], axis=0)
    time_turned = time_ref[...].T
    columns = high_ref.shape[1] // snapshots
    wide = PAIR * columns
    total = jnp.zeros((rank, columns), f32)
    for first in range(0, snapshots, PAIR):
        at = first * columns
        product = raw_dot(both, high_ref[:, at : at + wide], 1, 0)
        along = product[:rank] + product[rank:] + raw_dot(high, low_ref[:, at : at + wide], 1, 0)
        along_ref[:, at : at + wide] = along
        for k in range(PAIR):
            total = total + along[:, k * columns : (k + 1) * columns] * time_turned[:, first + k : first + k + 1]
    pack(out_ref, total.T, gram)


def third_product(in_ref, along_ref, gram_time_ref, out_ref, raw_ref, gram_ref, norm_ref):
    rank = gram_time_ref.shape[0]
    extra = rank // in_ref.shape[0]
    rows = in_ref.shape[1] - extra
    snapshots = out_ref.shape[1] - extra
    norm_row, norm_column, gram_a, ends = scaled(unpack(in_ref, rows, extra))
    gram_time = gram_time_ref[...]
    inverse = metric_inverse(gram_a, gram_time, ends, diagonal(gram_time))
    turned = dot(inverse, unpack(in_ref, 0, rows) / norm_row, 1, 1)
    raw_ref[...] = dot(in_ref[lax.axis_index("gx"), :rows, :] / norm_row, inverse, 1, 1)
    gram_ref[...] = gram_a
    norm_ref[...] = norm_row
    gram = dot(turned, turned, 1, 1)
    columns = turned.shape[1]
    lane = lax.broadcasted_iota(jnp.int32, (rank, rank), 1)
    sums = jnp.zeros((rank, rank), f32)
    for k in range(snapshots):
        part = jnp.sum(along_ref[:, k * columns : (k + 1) * columns] * turned, axis=1, keepdims=True)
        sums = jnp.where(lane == k, part, sums)
    products = (sums / norm_column).T[:snapshots]
    mine = gram_slice(gram, lax.axis_index("gx"), extra)
    for d in range(out_ref.shape[0]):
        out_ref[d, :snapshots, :] = products
        out_ref[d, snapshots:, :] = mine


def gram_slice(gram, index, extra):
    value = gram[:extra]
    for s in range(1, gram.shape[0] // extra):
        value = jnp.where(index == s, gram[s * extra : (s + 1) * extra], value)
    return value


def finish(size_a, size_b, in_ref, gram_a_ref, norm_a_ref, raw_a_ref, raw_b_ref, factor_a_ref, factor_b_ref, time_ref):
    snapshots = time_ref.shape[0]
    norm_row, _, gram_b, ends = scaled(unpack(in_ref, snapshots, in_ref.shape[1] - snapshots))
    gram_a = gram_a_ref[...]
    products = jnp.sum(in_ref[:, :snapshots, :], axis=0) / norm_row
    time_ref[...] = dot(products, metric_inverse(gram_b, gram_a, ends, diagonal(gram_a)), 1, 0)
    factor_a_ref[...] = raw_a_ref[...] / norm_a_ref[...] * jnp.sqrt(f32(size_a))
    factor_b_ref[...] = raw_b_ref[...] / norm_row * jnp.sqrt(f32(size_b))


def call(kernel, inputs, outputs, name, spaces=None, scratch=(), limit=16 << 20, cost=None):
    shapes = [o if isinstance(o, jax.ShapeDtypeStruct) else jax.ShapeDtypeStruct(o, f32) for o in outputs]
    single = len(shapes) == 1
    space = pl.BlockSpec(memory_space=VMEM)
    return pl.pallas_call(
        kernel,
        out_shape=shapes[0] if single else shapes,
        in_specs=spaces or [space] * len(inputs),
        out_specs=space if single else [space] * len(shapes),
        scratch_shapes=scratch,
        cost_estimate=cost,
        compiler_params=pltpu.CompilerParams(vmem_limit_bytes=limit),
        name=name,
    )(*inputs)


def exchange(value, axis):
    return lax.all_to_all(value, axis, 0, 0)


def shards(tensor, factor_b_init, time_init):
    nx, ny = lax.axis_size("gx"), lax.axis_size("gy")
    snapshots, rank = time_init.shape
    rows_i, rows_j = tensor.shape[1], tensor.shape[2]
    own_i, own_j = rows_i // ny, rows_j // nx
    extra_x, extra_y = rank // nx, rank // ny
    behind = pl.CostEstimate(flops=5 * 10**9, bytes_accessed=2 * factor_b_init.size * 4 * nx, transcendentals=0)
    block_b = call(spread, (factor_b_init,), [(nx,) + factor_b_init.shape], "spread", cost=behind)
    block_b = exchange(block_b, "gx")
    half = jax.ShapeDtypeStruct((rows_i, snapshots * rows_j), bf16)
    sent, high, low, gram_time = call(
        first_product,
        (tensor, block_b, time_init),
        [(ny, own_i + extra_y, rank), half, half, (rank, rank)],
        "first_product",
        limit=16 << 20,
    )
    sent = exchange(sent, "gy")
    sent = call(sum_and_copy, (sent,), [sent.shape], "sum_a")
    sent = exchange(sent, "gy")
    sent, along, raw_a = call(
        second_product,
        (high, low, sent, time_init, gram_time),
        [(nx, own_j + extra_x, rank), (rank, snapshots * rows_j), (own_i, rank)],
        "second_product",
    )
    sent = exchange(sent, "gx")
    sent = call(sum_and_copy, (sent,), [sent.shape], "sum_b")
    sent = exchange(sent, "gx")
    sent, raw_b, gram_a, norm_a = call(
        third_product,
        (sent, along, gram_time),
        [(ny, snapshots + extra_x, rank), (own_j, rank), (rank, rank), (1, rank)],
        "third_product",
    )
    sent = exchange(sent, "gy")
    sent = call(sum_and_copy, (sent,), [(nx,) + sent.shape[1:]], "sum_c")
    sent = exchange(sent, "gx")
    return call(
        functools.partial(finish, rows_i * nx, rows_j * ny),
        (sent, gram_a, norm_a, raw_a, raw_b),
        [(own_i, rank), (own_j, rank), (snapshots, rank)],
        "finish",
    )


def solution(mesh):
    return jax.shard_map(
        lambda *arrays: tuple(shards(*arrays)),
        mesh=mesh,
        in_specs=(P(None, "gx", "gy"), P(("gy", "gx"), None), P()),
        out_specs=(P(("gx", "gy"), None), P(("gy", "gx"), None), P()),
        check_vma=False,
    )
```

```python
import functools

import jax
import jax.numpy as jnp
from jax import lax
from jax.experimental import pallas as pl
from jax.experimental.pallas import tpu as pltpu
from jax.sharding import PartitionSpec as P

highest = lax.Precision.HIGHEST
epsilon = 1e-06
f32 = jnp.float32
bf16 = jnp.bfloat16
VMEM = pltpu.VMEM
TILE = 8
PAIR = 8
LOOK = 2


def split(x):
    high = x.astype(bf16)
    return high, (x - high.astype(f32)).astype(bf16)


def dot(a, b, ca, cb, precision=highest):
    return lax.dot_general(a, b, (((ca,), (cb,)), ((), ())), precision=precision, preferred_element_type=f32)


def raw_dot(a, b, ca, cb):
    return lax.dot_general(a, b, (((ca,), (cb,)), ((), ())), preferred_element_type=f32)


def three_parts(x):
    high = x.astype(bf16)
    rest = x - high.astype(f32)
    middle = rest.astype(bf16)
    return high, middle, (rest - middle.astype(f32)).astype(bf16)


def spd_inverse(matrix):
    n = matrix.shape[0]
    blocks = n // TILE
    rows = [matrix[TILE * v : TILE * (v + 1), :] for v in range(blocks)]
    lane = lax.broadcasted_iota(jnp.int32, (TILE, n), 1)
    sub = lax.broadcasted_iota(jnp.int32, (TILE, n), 0)
    zero = jnp.zeros((TILE, n), f32)

    def column(value, at):
        return jnp.take_along_axis(value, jnp.full((TILE, n), at, jnp.int32), axis=1)

    def row(value, at):
        return jnp.broadcast_to(value[at : at + 1, :], (TILE, n))

    for block in range(blocks):
        first = TILE * block
        inside = (lane >= first) & (lane < first + TILE)
        panel = rows[block]
        columns = [column(panel, first + s) for s in range(TILE)]
        b = [[row(columns[s], i) for s in range(i + 1)] for i in range(TILE)]
        start = jnp.where(inside, jnp.where(lane - first == sub, 1.0, 0.0), panel)
        p = [row(start, i) for i in range(TILE)]
        inverse = []
        for j in range(TILE):
            inverse.append(1.0 / b[j][j])
            for i in range(j + 1, TILE):
                factor = b[i][j] * inverse[j]
                for t in range(j + 1, i + 1):
                    b[i][t] = b[i][t] - factor * b[t][j]
                p[i] = p[i] - factor * p[j]
        solved = [None] * TILE
        for j in reversed(range(TILE)):
            value = p[j]
            for i in range(j + 1, TILE):
                value = value - b[i][j] * solved[i]
            solved[j] = value * inverse[j]
        result = solved[TILE - 1]
        for s in range(TILE - 1):
            result = jnp.where(sub == s, solved[s], result)
        c_high, c_middle, c_low = three_parts(jnp.concatenate(rows, axis=0))
        r_high, r_middle, r_low = [
            jnp.concatenate([part.astype(f32) if v == block else zero for v in range(blocks)], axis=0).astype(bf16)
            for part in three_parts(result)
        ]
        none = jnp.zeros_like(r_high)
        right = [(r_high, r_middle), (r_high, r_middle), (r_low, none), (r_high, none)]
        right = jnp.concatenate([jnp.concatenate(pair, axis=1) for pair in right], axis=0)
        product = raw_dot(jnp.concatenate([c_high, c_middle, c_high, c_low], axis=1), right, 1, 0)
        product = product[:, :n] + product[:, n:]
        near = [(block + 1 + q) % blocks for q in range(LOOK)]
        update = []
        for v in range(blocks):
            if v == block:
                update.append(result)
                continue
            if v in near:
                terms = [column(rows[v], first + s) * solved[s] for s in range(TILE)]
                while len(terms) > 1:
                    terms = [terms[q] + terms[q + 1] for q in range(0, len(terms), 2)]
                change = terms[0]
            else:
                change = product[TILE * v : TILE * (v + 1), :]
            update.append(jnp.where(inside, 0.0, rows[v]) - change)
        rows = update
    return jnp.concatenate(rows, axis=0)


def diagonal(matrix):
    n = matrix.shape[0]
    same = lax.broadcasted_iota(jnp.int32, (n, n), 0) == lax.broadcasted_iota(jnp.int32, (n, n), 1)
    kept = jnp.where(same, matrix, 0.0)
    return jnp.sum(kept, axis=0, keepdims=True), jnp.sum(kept, axis=1, keepdims=True)


def metric_inverse(one, other, one_diagonal, other_diagonal):
    across, down = [lax.rsqrt(p * q) for p, q in zip(one_diagonal, other_diagonal)]
    scale = down * across
    return spd_inverse(one * other * scale) * scale


def scaled(gram_raw):
    across, down = diagonal(gram_raw)
    norm_row, norm_column = jnp.sqrt(across + epsilon), jnp.sqrt(down + epsilon)
    ends = across / (norm_row * norm_row), down / (norm_column * norm_column)
    return norm_row, norm_column, gram_raw / (norm_column * norm_row), ends


def unpack(ref, at, size):
    return jnp.concatenate([ref[s, at : at + size, :] for s in range(ref.shape[0])], axis=0)


def spread(factor_ref, out_ref):
    for d in range(out_ref.shape[0]):
        out_ref[d] = factor_ref[...]


def first_product(tensor_ref, factor_ref, time_ref, out_ref, high_ref, low_ref, gram_time_ref):
    factor = unpack(factor_ref, 0, factor_ref.shape[1])
    columns, rank = factor.shape
    total = jnp.zeros((tensor_ref.shape[1], rank), f32)
    for first in range(0, time_ref.shape[0], PAIR):
        weights = jnp.concatenate([factor * time_ref[k : k + 1, :] for k in range(first, first + PAIR)], axis=0)
        high, low = split(weights)
        both = jnp.concatenate([high, low], axis=1)
        t_high, t_low = split(jnp.concatenate([tensor_ref[k] for k in range(first, first + PAIR)], axis=1))
        at = first * columns
        high_ref[:, at : at + PAIR * columns] = t_high
        low_ref[:, at : at + PAIR * columns] = t_low
        product = raw_dot(t_high, both, 1, 0)
        total = total + (product[:, :rank] + product[:, rank:] + raw_dot(t_low, high, 1, 0))
    gram = dot(factor, factor, 0, 0)
    pack(out_ref, total, gram)
    gram_time_ref[...] = dot(time_ref[...], time_ref[...], 0, 0)


def pack(out_ref, total, gram):
    parts = out_ref.shape[0]
    rows, extra = total.shape[0] // parts, gram.shape[0] // parts
    for d in range(parts):
        out_ref[d, :rows, :] = total[d * rows : (d + 1) * rows]
        out_ref[d, rows:, :] = gram[d * extra : (d + 1) * extra]


def sum_and_copy(in_ref, out_ref):
    total = jnp.sum(in_ref[...], axis=0)
    for d in range(out_ref.shape[0]):
        out_ref[d] = total


def second_product(high_ref, low_ref, in_ref, time_ref, gram_time_ref, out_ref, along_ref, raw_ref):
    snapshots, rank = time_ref.shape
    rows = in_ref.shape[1] - rank // in_ref.shape[0]
    gram_old, gram_time = unpack(in_ref, rows, in_ref.shape[1] - rows), gram_time_ref[...]
    inverse = metric_inverse(gram_old, gram_time, diagonal(gram_old), diagonal(gram_time))
    turned = dot(inverse, unpack(in_ref, 0, rows), 1, 1)
    raw_ref[...] = dot(in_ref[lax.axis_index("gy"), :rows, :], inverse, 1, 1)
    gram = dot(turned, turned, 1, 1)
    high, low = split(turned)
    both = jnp.concatenate([high, low], axis=0)
    time_turned = time_ref[...].T
    columns = high_ref.shape[1] // snapshots
    wide = PAIR * columns
    total = jnp.zeros((rank, columns), f32)
    for first in range(0, snapshots, PAIR):
        at = first * columns
        product = raw_dot(both, high_ref[:, at : at + wide], 1, 0)
        along = product[:rank] + product[rank:] + raw_dot(high, low_ref[:, at : at + wide], 1, 0)
        along_ref[:, at : at + wide] = along
        for k in range(PAIR):
            total = total + along[:, k * columns : (k + 1) * columns] * time_turned[:, first + k : first + k + 1]
    pack(out_ref, total.T, gram)


def third_product(in_ref, along_ref, gram_time_ref, out_ref, raw_ref, gram_ref, norm_ref):
    rank = gram_time_ref.shape[0]
    extra = rank // in_ref.shape[0]
    rows = in_ref.shape[1] - extra
    snapshots = out_ref.shape[1] - extra
    norm_row, norm_column, gram_a, ends = scaled(unpack(in_ref, rows, extra))
    gram_time = gram_time_ref[...]
    inverse = metric_inverse(gram_a, gram_time, ends, diagonal(gram_time))
    turned = dot(inverse, unpack(in_ref, 0, rows) / norm_row, 1, 1)
    raw_ref[...] = dot(in_ref[lax.axis_index("gx"), :rows, :] / norm_row, inverse, 1, 1)
    gram_ref[...] = gram_a
    norm_ref[...] = norm_row
    gram = dot(turned, turned, 1, 1)
    columns = turned.shape[1]
    lane = lax.broadcasted_iota(jnp.int32, (rank, rank), 1)
    sums = jnp.zeros((rank, rank), f32)
    for k in range(snapshots):
        part = jnp.sum(along_ref[:, k * columns : (k + 1) * columns] * turned, axis=1, keepdims=True)
        sums = jnp.where(lane == k, part, sums)
    products = (sums / norm_column).T[:snapshots]
    mine = gram_slice(gram, lax.axis_index("gx"), extra)
    for d in range(out_ref.shape[0]):
        out_ref[d, :snapshots, :] = products
        out_ref[d, snapshots:, :] = mine


def gram_slice(gram, index, extra):
    value = gram[:extra]
    for s in range(1, gram.shape[0] // extra):
        value = jnp.where(index == s, gram[s * extra : (s + 1) * extra], value)
    return value


def finish(size_a, size_b, in_ref, gram_a_ref, norm_a_ref, raw_a_ref, raw_b_ref, factor_a_ref, factor_b_ref, time_ref):
    snapshots = time_ref.shape[0]
    norm_row, _, gram_b, ends = scaled(unpack(in_ref, snapshots, in_ref.shape[1] - snapshots))
    gram_a = gram_a_ref[...]
    products = jnp.sum(in_ref[:, :snapshots, :], axis=0) / norm_row
    time_ref[...] = dot(products, metric_inverse(gram_b, gram_a, ends, diagonal(gram_a)), 1, 0)
    factor_a_ref[...] = raw_a_ref[...] / norm_a_ref[...] * jnp.sqrt(f32(size_a))
    factor_b_ref[...] = raw_b_ref[...] / norm_row * jnp.sqrt(f32(size_b))


def call(kernel, inputs, outputs, name, spaces=None, scratch=(), limit=16 << 20, cost=None):
    shapes = [o if isinstance(o, jax.ShapeDtypeStruct) else jax.ShapeDtypeStruct(o, f32) for o in outputs]
    single = len(shapes) == 1
    space = pl.BlockSpec(memory_space=VMEM)
    return pl.pallas_call(
        kernel,
        out_shape=shapes[0] if single else shapes,
        in_specs=spaces or [space] * len(inputs),
        out_specs=space if single else [space] * len(shapes),
        scratch_shapes=scratch,
        cost_estimate=cost,
        compiler_params=pltpu.CompilerParams(vmem_limit_bytes=limit),
        name=name,
    )(*inputs)


def exchange(value, axis):
    return lax.all_to_all(value, axis, 0, 0)


def shards(tensor, factor_b_init, time_init):
    nx, ny = lax.axis_size("gx"), lax.axis_size("gy")
    snapshots, rank = time_init.shape
    rows_i, rows_j = tensor.shape[1], tensor.shape[2]
    own_i, own_j = rows_i // ny, rows_j // nx
    extra_x, extra_y = rank // nx, rank // ny
    behind = pl.CostEstimate(flops=5 * 10**9, bytes_accessed=2 * factor_b_init.size * 4 * nx, transcendentals=0)
    block_b = call(spread, (factor_b_init,), [(nx,) + factor_b_init.shape], "spread", cost=behind)
    block_b = exchange(block_b, "gx")
    half = jax.ShapeDtypeStruct((rows_i, snapshots * rows_j), bf16)
    sent, high, low, gram_time = call(
        first_product,
        (tensor, block_b, time_init),
        [(ny, own_i + extra_y, rank), half, half, (rank, rank)],
        "first_product",
        limit=16 << 20,
    )
    sent = exchange(sent, "gy")
    sent = call(sum_and_copy, (sent,), [sent.shape], "sum_a")
    sent = exchange(sent, "gy")
    sent, along, raw_a = call(
        second_product,
        (high, low, sent, time_init, gram_time),
        [(nx, own_j + extra_x, rank), (rank, snapshots * rows_j), (own_i, rank)],
        "second_product",
    )
    sent = exchange(sent, "gx")
    sent = call(sum_and_copy, (sent,), [sent.shape], "sum_b")
    sent = exchange(sent, "gx")
    sent, raw_b, gram_a, norm_a = call(
        third_product,
        (sent, along, gram_time),
        [(ny, snapshots + extra_x, rank), (own_j, rank), (rank, rank), (1, rank)],
        "third_product",
    )
    sent = exchange(sent, "gy")
    sent = call(sum_and_copy, (sent,), [(nx,) + sent.shape[1:]], "sum_c")
    sent = exchange(sent, "gx")
    return call(
        functools.partial(finish, rows_i * nx, rows_j * ny),
        (sent, gram_a, norm_a, raw_a, raw_b),
        [(own_i, rank), (own_j, rank), (snapshots, rank)],
        "finish",
    )


def solution(mesh):
    return jax.shard_map(
        lambda *arrays: tuple(shards(*arrays)),
        mesh=mesh,
        in_specs=(P(None, "gx", "gy"), P(("gy", "gx"), None), P()),
        out_specs=(P(("gx", "gy"), None), P(("gy", "gx"), None), P()),
        check_vma=False,
    )
```

```python
import functools

import jax
import jax.numpy as jnp
from jax import lax
from jax.experimental import pallas as pl
from jax.experimental.pallas import tpu as pltpu
from jax.sharding import PartitionSpec as P

highest = lax.Precision.HIGHEST
epsilon = 1e-06
f32 = jnp.float32
bf16 = jnp.bfloat16
VMEM = pltpu.VMEM
TILE = 8
PAIR = 8
LOOK = 2


def split(x):
    high = x.astype(bf16)
    return high, (x - high.astype(f32)).astype(bf16)


def dot(a, b, ca, cb, precision=highest):
    return lax.dot_general(a, b, (((ca,), (cb,)), ((), ())), precision=precision, preferred_element_type=f32)


def raw_dot(a, b, ca, cb):
    return lax.dot_general(a, b, (((ca,), (cb,)), ((), ())), preferred_element_type=f32)


def three_parts(x):
    high = x.astype(bf16)
    rest = x - high.astype(f32)
    middle = rest.astype(bf16)
    return high, middle, (rest - middle.astype(f32)).astype(bf16)


def spd_inverse(matrix):
    n = matrix.shape[0]
    blocks = n // TILE
    rows = [matrix[TILE * v : TILE * (v + 1), :] for v in range(blocks)]
    lane = lax.broadcasted_iota(jnp.int32, (TILE, n), 1)
    sub = lax.broadcasted_iota(jnp.int32, (TILE, n), 0)
    zero = jnp.zeros((TILE, n), f32)

    def column(value, at):
        return jnp.take_along_axis(value, jnp.full((TILE, n), at, jnp.int32), axis=1)

    def row(value, at):
        return jnp.broadcast_to(value[at : at + 1, :], (TILE, n))

    for block in range(blocks):
        first = TILE * block
        inside = (lane >= first) & (lane < first + TILE)
        panel = rows[block]
        columns = [column(panel, first + s) for s in range(TILE)]
        b = [[row(columns[s], i) for s in range(i + 1)] for i in range(TILE)]
        start = jnp.where(inside, jnp.where(lane - first == sub, 1.0, 0.0), panel)
        p = [row(start, i) for i in range(TILE)]
        inverse = []
        for j in range(TILE):
            inverse.append(1.0 / b[j][j])
            for i in range(j + 1, TILE):
                factor = b[i][j] * inverse[j]
                for t in range(j + 1, i + 1):
                    b[i][t] = b[i][t] - factor * b[t][j]
                p[i] = p[i] - factor * p[j]
        solved = [None] * TILE
        for j in reversed(range(TILE)):
            value = p[j]
            for i in range(j + 1, TILE):
                value = value - b[i][j] * solved[i]
            solved[j] = value * inverse[j]
        result = solved[TILE - 1]
        for s in range(TILE - 1):
            result = jnp.where(sub == s, solved[s], result)
        c_high, c_middle, c_low = three_parts(jnp.concatenate(rows, axis=0))
        r_high, r_middle, r_low = [
            jnp.concatenate([part.astype(f32) if v == block else zero for v in range(blocks)], axis=0).astype(bf16)
            for part in three_parts(result)
        ]
        none = jnp.zeros_like(r_high)
        right = [(r_high, r_middle), (r_high, r_middle), (r_low, none), (r_high, none)]
        right = jnp.concatenate([jnp.concatenate(pair, axis=1) for pair in right], axis=0)
        product = raw_dot(jnp.concatenate([c_high, c_middle, c_high, c_low], axis=1), right, 1, 0)
        product = product[:, :n] + product[:, n:]
        near = [(block + 1 + q) % blocks for q in range(LOOK)]
        update = []
        for v in range(blocks):
            if v == block:
                update.append(result)
                continue
            if v in near:
                terms = [column(rows[v], first + s) * solved[s] for s in range(TILE)]
                while len(terms) > 1:
                    terms = [terms[q] + terms[q + 1] for q in range(0, len(terms), 2)]
                change = terms[0]
            else:
                change = product[TILE * v : TILE * (v + 1), :]
            update.append(jnp.where(inside, 0.0, rows[v]) - change)
        rows = update
    return jnp.concatenate(rows, axis=0)


def diagonal(matrix):
    n = matrix.shape[0]
    same = lax.broadcasted_iota(jnp.int32, (n, n), 0) == lax.broadcasted_iota(jnp.int32, (n, n), 1)
    kept = jnp.where(same, matrix, 0.0)
    return jnp.sum(kept, axis=0, keepdims=True), jnp.sum(kept, axis=1, keepdims=True)


def metric_inverse(one, other, one_diagonal, other_diagonal):
    across, down = [lax.rsqrt(p * q) for p, q in zip(one_diagonal, other_diagonal)]
    scale = down * across
    return spd_inverse(one * other * scale) * scale


def scaled(gram_raw):
    across, down = diagonal(gram_raw)
    norm_row, norm_column = jnp.sqrt(across + epsilon), jnp.sqrt(down + epsilon)
    ends = across / (norm_row * norm_row), down / (norm_column * norm_column)
    return norm_row, norm_column, gram_raw / (norm_column * norm_row), ends


def unpack(ref, at, size):
    return jnp.concatenate([ref[s, at : at + size, :] for s in range(ref.shape[0])], axis=0)


def spread(factor_ref, out_ref):
    for d in range(out_ref.shape[0]):
        out_ref[d] = factor_ref[...]


def first_product(tensor_ref, factor_ref, time_ref, out_ref, high_ref, low_ref, gram_time_ref):
    factor = unpack(factor_ref, 0, factor_ref.shape[1])
    columns, rank = factor.shape
    total = jnp.zeros((tensor_ref.shape[1], rank), f32)
    for first in range(0, time_ref.shape[0], PAIR):
        weights = jnp.concatenate([factor * time_ref[k : k + 1, :] for k in range(first, first + PAIR)], axis=0)
        high, low = split(weights)
        both = jnp.concatenate([high, low], axis=1)
        t_high, t_low = split(jnp.concatenate([tensor_ref[k] for k in range(first, first + PAIR)], axis=1))
        at = first * columns
        high_ref[:, at : at + PAIR * columns] = t_high
        low_ref[:, at : at + PAIR * columns] = t_low
        product = raw_dot(t_high, both, 1, 0)
        total = total + (product[:, :rank] + product[:, rank:] + raw_dot(t_low, high, 1, 0))
    gram = dot(factor, factor, 0, 0)
    pack(out_ref, total, gram)
    gram_time_ref[...] = dot(time_ref[...], time_ref[...], 0, 0)


def pack(out_ref, total, gram):
    parts = out_ref.shape[0]
    rows, extra = total.shape[0] // parts, gram.shape[0] // parts
    for d in range(parts):
        out_ref[d, :rows, :] = total[d * rows : (d + 1) * rows]
        out_ref[d, rows:, :] = gram[d * extra : (d + 1) * extra]


def sum_and_copy(in_ref, out_ref):
    total = jnp.sum(in_ref[...], axis=0)
    for d in range(out_ref.shape[0]):
        out_ref[d] = total


def second_product(high_ref, low_ref, in_ref, time_ref, gram_time_ref, out_ref, along_ref, own_ref, inverse_ref):
    snapshots, rank = time_ref.shape
    rows = in_ref.shape[1] - rank // in_ref.shape[0]
    gram_old, gram_time = unpack(in_ref, rows, in_ref.shape[1] - rows), gram_time_ref[...]
    inverse = metric_inverse(gram_old, gram_time, diagonal(gram_old), diagonal(gram_time))
    turned = dot(inverse, unpack(in_ref, 0, rows), 1, 1)
    own_ref[...] = in_ref[lax.axis_index("gy"), :rows, :]
    inverse_ref[...] = inverse
    gram = dot(turned, turned, 1, 1)
    high, low = split(turned)
    both = jnp.concatenate([high, low], axis=0)
    time_turned = time_ref[...].T
    columns = high_ref.shape[1] // snapshots
    wide = PAIR * columns
    total = jnp.zeros((rank, columns), f32)
    for first in range(0, snapshots, PAIR):
        at = first * columns
        product = raw_dot(both, high_ref[:, at : at + wide], 1, 0)
        along = product[:rank] + product[rank:] + raw_dot(high, low_ref[:, at : at + wide], 1, 0)
        along_ref[:, at : at + wide] = along
        for k in range(PAIR):
            total = total + along[:, k * columns : (k + 1) * columns] * time_turned[:, first + k : first + k + 1]
    pack(out_ref, total.T, gram)


def third_product(in_ref, along_ref, gram_time_ref, out_ref, own_ref, inverse_ref, gram_ref, norm_ref):
    rank = gram_time_ref.shape[0]
    extra = rank // in_ref.shape[0]
    rows = in_ref.shape[1] - extra
    snapshots = out_ref.shape[1] - extra
    norm_row, norm_column, gram_a, ends = scaled(unpack(in_ref, rows, extra))
    gram_time = gram_time_ref[...]
    inverse = metric_inverse(gram_a, gram_time, ends, diagonal(gram_time))
    turned = dot(inverse, unpack(in_ref, 0, rows) / norm_row, 1, 1)
    own_ref[...] = in_ref[lax.axis_index("gx"), :rows, :] / norm_row
    inverse_ref[...] = inverse
    gram_ref[...] = gram_a
    norm_ref[...] = norm_row
    gram = dot(turned, turned, 1, 1)
    columns = turned.shape[1]
    lane = lax.broadcasted_iota(jnp.int32, (rank, rank), 1)
    sums = jnp.zeros((rank, rank), f32)
    for k in range(snapshots):
        part = jnp.sum(along_ref[:, k * columns : (k + 1) * columns] * turned, axis=1, keepdims=True)
        sums = jnp.where(lane == k, part, sums)
    products = (sums / norm_column).T[:snapshots]
    mine = gram_slice(gram, lax.axis_index("gx"), extra)
    for d in range(out_ref.shape[0]):
        out_ref[d, :snapshots, :] = products
        out_ref[d, snapshots:, :] = mine


def gram_slice(gram, index, extra):
    value = gram[:extra]
    for s in range(1, gram.shape[0] // extra):
        value = jnp.where(index == s, gram[s * extra : (s + 1) * extra], value)
    return value


def finish(size_a, size_b, in_ref, gram_a_ref, norm_a_ref, own_a_ref, inverse_a_ref, own_b_ref, inverse_b_ref, factor_a_ref, factor_b_ref, time_ref):
    snapshots = time_ref.shape[0]
    norm_row, _, gram_b, ends = scaled(unpack(in_ref, snapshots, in_ref.shape[1] - snapshots))
    gram_a = gram_a_ref[...]
    products = jnp.sum(in_ref[:, :snapshots, :], axis=0) / norm_row
    raw_a = dot(own_a_ref[...], inverse_a_ref[...], 1, 1)
    raw_b = dot(own_b_ref[...], inverse_b_ref[...], 1, 1)
    factor_a_ref[...] = raw_a / norm_a_ref[...] * jnp.sqrt(f32(size_a))
    factor_b_ref[...] = raw_b / norm_row * jnp.sqrt(f32(size_b))
    time_ref[...] = dot(products, metric_inverse(gram_b, gram_a, ends, diagonal(gram_a)), 1, 0)


def call(kernel, inputs, outputs, name, spaces=None, scratch=(), limit=16 << 20, cost=None):
    shapes = [o if isinstance(o, jax.ShapeDtypeStruct) else jax.ShapeDtypeStruct(o, f32) for o in outputs]
    single = len(shapes) == 1
    space = pl.BlockSpec(memory_space=VMEM)
    return pl.pallas_call(
        kernel,
        out_shape=shapes[0] if single else shapes,
        in_specs=spaces or [space] * len(inputs),
        out_specs=space if single else [space] * len(shapes),
        scratch_shapes=scratch,
        cost_estimate=cost,
        compiler_params=pltpu.CompilerParams(vmem_limit_bytes=limit),
        name=name,
    )(*inputs)


def exchange(value, axis):
    return lax.all_to_all(value, axis, 0, 0)


def shards(tensor, factor_b_init, time_init):
    nx, ny = lax.axis_size("gx"), lax.axis_size("gy")
    snapshots, rank = time_init.shape
    rows_i, rows_j = tensor.shape[1], tensor.shape[2]
    own_i, own_j = rows_i // ny, rows_j // nx
    extra_x, extra_y = rank // nx, rank // ny
    behind = pl.CostEstimate(flops=5 * 10**9, bytes_accessed=2 * factor_b_init.size * 4 * nx, transcendentals=0)
    block_b = call(spread, (factor_b_init,), [(nx,) + factor_b_init.shape], "spread", cost=behind)
    block_b = exchange(block_b, "gx")
    half = jax.ShapeDtypeStruct((rows_i, snapshots * rows_j), bf16)
    sent, high, low, gram_time = call(
        first_product,
        (tensor, block_b, time_init),
        [(ny, own_i + extra_y, rank), half, half, (rank, rank)],
        "first_product",
        limit=16 << 20,
    )
    sent = exchange(sent, "gy")
    sent = call(sum_and_copy, (sent,), [sent.shape], "sum_a")
    sent = exchange(sent, "gy")
    sent, along, own_a, inverse_a = call(
        second_product,
        (high, low, sent, time_init, gram_time),
        [(nx, own_j + extra_x, rank), (rank, snapshots * rows_j), (own_i, rank), (rank, rank)],
        "second_product",
    )
    sent = exchange(sent, "gx")
    sent = call(sum_and_copy, (sent,), [sent.shape], "sum_b")
    sent = exchange(sent, "gx")
    sent, own_b, inverse_b, gram_a, norm_a = call(
        third_product,
        (sent, along, gram_time),
        [(ny, snapshots + extra_x, rank), (own_j, rank), (rank, rank), (rank, rank), (1, rank)],
        "third_product",
    )
    sent = exchange(sent, "gy")
    sent = call(sum_and_copy, (sent,), [(nx,) + sent.shape[1:]], "sum_c")
    sent = exchange(sent, "gx")
    return call(
        functools.partial(finish, rows_i * nx, rows_j * ny),
        (sent, gram_a, norm_a, own_a, inverse_a, own_b, inverse_b),
        [(own_i, rank), (own_j, rank), (snapshots, rank)],
        "finish",
    )


def solution(mesh):
    return jax.shard_map(
        lambda *arrays: tuple(shards(*arrays)),
        mesh=mesh,
        in_specs=(P(None, "gx", "gy"), P(("gy", "gx"), None), P()),
        out_specs=(P(("gx", "gy"), None), P(("gy", "gx"), None), P()),
        check_vma=False,
    )
```

```python
import functools

import jax
import jax.numpy as jnp
from jax import lax
from jax.experimental import pallas as pl
from jax.experimental.pallas import tpu as pltpu
from jax.sharding import PartitionSpec as P

highest = lax.Precision.HIGHEST
epsilon = 1e-06
f32 = jnp.float32
bf16 = jnp.bfloat16
VMEM = pltpu.VMEM
TILE = 8
PAIR = 8
LOOK = 2


def split(x):
    high = x.astype(bf16)
    return high, (x - high.astype(f32)).astype(bf16)


def dot(a, b, ca, cb, precision=highest):
    return lax.dot_general(a, b, (((ca,), (cb,)), ((), ())), precision=precision, preferred_element_type=f32)


def raw_dot(a, b, ca, cb):
    return lax.dot_general(a, b, (((ca,), (cb,)), ((), ())), preferred_element_type=f32)


def three_parts(x):
    high = x.astype(bf16)
    rest = x - high.astype(f32)
    middle = rest.astype(bf16)
    return high, middle, (rest - middle.astype(f32)).astype(bf16)


def spd_inverse(matrix):
    n = matrix.shape[0]
    blocks = n // TILE
    rows = [matrix[TILE * v : TILE * (v + 1), :] for v in range(blocks)]
    lane = lax.broadcasted_iota(jnp.int32, (TILE, n), 1)
    sub = lax.broadcasted_iota(jnp.int32, (TILE, n), 0)
    zero = jnp.zeros((TILE, n), f32)

    def column(value, at):
        return jnp.take_along_axis(value, jnp.full((TILE, n), at, jnp.int32), axis=1)

    def row(value, at):
        return jnp.broadcast_to(value[at : at + 1, :], (TILE, n))

    for block in range(blocks):
        first = TILE * block
        inside = (lane >= first) & (lane < first + TILE)
        panel = rows[block]
        columns = [column(panel, first + s) for s in range(TILE)]
        b = [[row(columns[s], i) for s in range(i + 1)] for i in range(TILE)]
        start = jnp.where(inside, jnp.where(lane - first == sub, 1.0, 0.0), panel)
        p = [row(start, i) for i in range(TILE)]
        inverse = []
        for j in range(TILE):
            inverse.append(1.0 / b[j][j])
            for i in range(j + 1, TILE):
                factor = b[i][j] * inverse[j]
                for t in range(j + 1, i + 1):
                    b[i][t] = b[i][t] - factor * b[t][j]
                p[i] = p[i] - factor * p[j]
        solved = [None] * TILE
        for j in reversed(range(TILE)):
            value = p[j]
            for i in range(j + 1, TILE):
                value = value - b[i][j] * solved[i]
            solved[j] = value * inverse[j]
        result = solved[TILE - 1]
        for s in range(TILE - 1):
            result = jnp.where(sub == s, solved[s], result)
        c_high, c_middle, c_low = three_parts(jnp.concatenate(rows, axis=0))
        r_high, r_middle, r_low = [
            jnp.concatenate([part.astype(f32) if v == block else zero for v in range(blocks)], axis=0).astype(bf16)
            for part in three_parts(result)
        ]
        none = jnp.zeros_like(r_high)
        right = [(r_high, r_middle), (r_high, r_middle), (r_low, none), (r_high, none)]
        right = jnp.concatenate([jnp.concatenate(pair, axis=1) for pair in right], axis=0)
        product = raw_dot(jnp.concatenate([c_high, c_middle, c_high, c_low], axis=1), right, 1, 0)
        product = product[:, :n] + product[:, n:]
        near = [(block + 1 + q) % blocks for q in range(LOOK)]
        update = []
        for v in range(blocks):
            if v == block:
                update.append(result)
                continue
            if v in near:
                terms = [column(rows[v], first + s) * solved[s] for s in range(TILE)]
                while len(terms) > 1:
                    terms = [terms[q] + terms[q + 1] for q in range(0, len(terms), 2)]
                change = terms[0]
            else:
                change = product[TILE * v : TILE * (v + 1), :]
            update.append(jnp.where(inside, 0.0, rows[v]) - change)
        rows = update
    return jnp.concatenate(rows, axis=0)


def diagonal(matrix):
    n = matrix.shape[0]
    same = lax.broadcasted_iota(jnp.int32, (n, n), 0) == lax.broadcasted_iota(jnp.int32, (n, n), 1)
    kept = jnp.where(same, matrix, 0.0)
    return jnp.sum(kept, axis=0, keepdims=True), jnp.sum(kept, axis=1, keepdims=True)


def metric_inverse(one, other, one_diagonal, other_diagonal):
    across, down = [lax.rsqrt(p * q) for p, q in zip(one_diagonal, other_diagonal)]
    scale = down * across
    return spd_inverse(one * other * scale) * scale


def scaled(gram_raw):
    across, down = diagonal(gram_raw)
    norm_row, norm_column = jnp.sqrt(across + epsilon), jnp.sqrt(down + epsilon)
    ends = across / (norm_row * norm_row), down / (norm_column * norm_column)
    return norm_row, norm_column, gram_raw * ((1.0 / norm_column) * (1.0 / norm_row)), ends


def unpack(ref, at, size):
    return jnp.concatenate([ref[s, at : at + size, :] for s in range(ref.shape[0])], axis=0)


def spread(factor_ref, out_ref):
    for d in range(out_ref.shape[0]):
        out_ref[d] = factor_ref[...]


def first_product(tensor_ref, factor_ref, time_ref, out_ref, high_ref, low_ref, gram_time_ref):
    factor = unpack(factor_ref, 0, factor_ref.shape[1])
    columns, rank = factor.shape
    total = jnp.zeros((tensor_ref.shape[1], rank), f32)
    for first in range(0, time_ref.shape[0], PAIR):
        weights = jnp.concatenate([factor * time_ref[k : k + 1, :] for k in range(first, first + PAIR)], axis=0)
        high, low = split(weights)
        both = jnp.concatenate([high, low], axis=1)
        t_high, t_low = split(jnp.concatenate([tensor_ref[k] for k in range(first, first + PAIR)], axis=1))
        at = first * columns
        high_ref[:, at : at + PAIR * columns] = t_high
        low_ref[:, at : at + PAIR * columns] = t_low
        product = raw_dot(t_high, both, 1, 0)
        total = total + (product[:, :rank] + product[:, rank:] + raw_dot(t_low, high, 1, 0))
    gram = dot(factor, factor, 0, 0)
    pack(out_ref, total, gram)
    gram_time_ref[...] = dot(time_ref[...], time_ref[...], 0, 0)


def pack(out_ref, total, gram):
    parts = out_ref.shape[0]
    rows, extra = total.shape[0] // parts, gram.shape[0] // parts
    for d in range(parts):
        out_ref[d, :rows, :] = total[d * rows : (d + 1) * rows]
        out_ref[d, rows:, :] = gram[d * extra : (d + 1) * extra]


def sum_and_copy(in_ref, out_ref):
    total = jnp.sum(in_ref[...], axis=0)
    for d in range(out_ref.shape[0]):
        out_ref[d] = total


def second_product(high_ref, low_ref, in_ref, time_ref, gram_time_ref, out_ref, along_ref, raw_ref):
    snapshots, rank = time_ref.shape
    rows = in_ref.shape[1] - rank // in_ref.shape[0]
    gram_old, gram_time = unpack(in_ref, rows, in_ref.shape[1] - rows), gram_time_ref[...]
    inverse = metric_inverse(gram_old, gram_time, diagonal(gram_old), diagonal(gram_time))
    turned = dot(inverse, unpack(in_ref, 0, rows), 1, 1)
    raw_ref[...] = dot(in_ref[lax.axis_index("gy"), :rows, :], inverse, 1, 1)
    gram = dot(turned, turned, 1, 1)
    high, low = split(turned)
    both = jnp.concatenate([high, low], axis=0)
    time_turned = time_ref[...].T
    columns = high_ref.shape[1] // snapshots
    wide = PAIR * columns
    total = jnp.zeros((rank, columns), f32)
    for first in range(0, snapshots, PAIR):
        at = first * columns
        product = raw_dot(both, high_ref[:, at : at + wide], 1, 0)
        along = product[:rank] + product[rank:] + raw_dot(high, low_ref[:, at : at + wide], 1, 0)
        along_ref[:, at : at + wide] = along
        for k in range(PAIR):
            total = total + along[:, k * columns : (k + 1) * columns] * time_turned[:, first + k : first + k + 1]
    pack(out_ref, total.T, gram)


def third_product(in_ref, along_ref, gram_time_ref, out_ref, raw_ref, gram_ref, norm_ref):
    rank = gram_time_ref.shape[0]
    extra = rank // in_ref.shape[0]
    rows = in_ref.shape[1] - extra
    snapshots = out_ref.shape[1] - extra
    norm_row, norm_column, gram_a, ends = scaled(unpack(in_ref, rows, extra))
    gram_time = gram_time_ref[...]
    inverse = metric_inverse(gram_a, gram_time, ends, diagonal(gram_time))
    turned = dot(inverse, unpack(in_ref, 0, rows) * (1.0 / norm_row), 1, 1)
    raw_ref[...] = dot(in_ref[lax.axis_index("gx"), :rows, :] * (1.0 / norm_row), inverse, 1, 1)
    gram_ref[...] = gram_a
    norm_ref[...] = norm_row
    gram = dot(turned, turned, 1, 1)
    columns = turned.shape[1]
    lane = lax.broadcasted_iota(jnp.int32, (rank, rank), 1)
    sums = jnp.zeros((rank, rank), f32)
    for k in range(snapshots):
        part = jnp.sum(along_ref[:, k * columns : (k + 1) * columns] * turned, axis=1, keepdims=True)
        sums = jnp.where(lane == k, part, sums)
    products = (sums / norm_column).T[:snapshots]
    mine = gram_slice(gram, lax.axis_index("gx"), extra)
    for d in range(out_ref.shape[0]):
        out_ref[d, :snapshots, :] = products
        out_ref[d, snapshots:, :] = mine


def gram_slice(gram, index, extra):
    value = gram[:extra]
    for s in range(1, gram.shape[0] // extra):
        value = jnp.where(index == s, gram[s * extra : (s + 1) * extra], value)
    return value


def finish(size_a, size_b, in_ref, gram_a_ref, norm_a_ref, raw_a_ref, raw_b_ref, factor_a_ref, factor_b_ref, time_ref):
    snapshots = time_ref.shape[0]
    norm_row, _, gram_b, ends = scaled(unpack(in_ref, snapshots, in_ref.shape[1] - snapshots))
    gram_a = gram_a_ref[...]
    products = jnp.sum(in_ref[:, :snapshots, :], axis=0) / norm_row
    time_ref[...] = dot(products, metric_inverse(gram_b, gram_a, ends, diagonal(gram_a)), 1, 0)
    factor_a_ref[...] = raw_a_ref[...] / norm_a_ref[...] * jnp.sqrt(f32(size_a))
    factor_b_ref[...] = raw_b_ref[...] / norm_row * jnp.sqrt(f32(size_b))


def call(kernel, inputs, outputs, name, spaces=None, scratch=(), limit=16 << 20, cost=None):
    shapes = [o if isinstance(o, jax.ShapeDtypeStruct) else jax.ShapeDtypeStruct(o, f32) for o in outputs]
    single = len(shapes) == 1
    space = pl.BlockSpec(memory_space=VMEM)
    return pl.pallas_call(
        kernel,
        out_shape=shapes[0] if single else shapes,
        in_specs=spaces or [space] * len(inputs),
        out_specs=space if single else [space] * len(shapes),
        scratch_shapes=scratch,
        cost_estimate=cost,
        compiler_params=pltpu.CompilerParams(vmem_limit_bytes=limit),
        name=name,
    )(*inputs)


def exchange(value, axis):
    return lax.all_to_all(value, axis, 0, 0)


def shards(tensor, factor_b_init, time_init):
    nx, ny = lax.axis_size("gx"), lax.axis_size("gy")
    snapshots, rank = time_init.shape
    rows_i, rows_j = tensor.shape[1], tensor.shape[2]
    own_i, own_j = rows_i // ny, rows_j // nx
    extra_x, extra_y = rank // nx, rank // ny
    behind = pl.CostEstimate(flops=5 * 10**9, bytes_accessed=2 * factor_b_init.size * 4 * nx, transcendentals=0)
    block_b = call(spread, (factor_b_init,), [(nx,) + factor_b_init.shape], "spread", cost=behind)
    block_b = exchange(block_b, "gx")
    half = jax.ShapeDtypeStruct((rows_i, snapshots * rows_j), bf16)
    sent, high, low, gram_time = call(
        first_product,
        (tensor, block_b, time_init),
        [(ny, own_i + extra_y, rank), half, half, (rank, rank)],
        "first_product",
        limit=16 << 20,
    )
    sent = exchange(sent, "gy")
    sent = call(sum_and_copy, (sent,), [sent.shape], "sum_a")
    sent = exchange(sent, "gy")
    sent, along, raw_a = call(
        second_product,
        (high, low, sent, time_init, gram_time),
        [(nx, own_j + extra_x, rank), (rank, snapshots * rows_j), (own_i, rank)],
        "second_product",
    )
    sent = exchange(sent, "gx")
    sent = call(sum_and_copy, (sent,), [sent.shape], "sum_b")
    sent = exchange(sent, "gx")
    sent, raw_b, gram_a, norm_a = call(
        third_product,
        (sent, along, gram_time),
        [(ny, snapshots + extra_x, rank), (own_j, rank), (rank, rank), (1, rank)],
        "third_product",
    )
    sent = exchange(sent, "gy")
    sent = call(sum_and_copy, (sent,), [(nx,) + sent.shape[1:]], "sum_c")
    sent = exchange(sent, "gx")
    return call(
        functools.partial(finish, rows_i * nx, rows_j * ny),
        (sent, gram_a, norm_a, raw_a, raw_b),
        [(own_i, rank), (own_j, rank), (snapshots, rank)],
        "finish",
    )


def solution(mesh):
    return jax.shard_map(
        lambda *arrays: tuple(shards(*arrays)),
        mesh=mesh,
        in_specs=(P(None, "gx", "gy"), P(("gy", "gx"), None), P()),
        out_specs=(P(("gx", "gy"), None), P(("gy", "gx"), None), P()),
        check_vma=False,
    )
```
